256 devices in a mesh: row: 16 (over x_lo, y, core), col: 16 (over z, x_hi).
Axes of the slice: x: 4 (x_hi: 2, x_lo: 2; x = x_hi * 2 + x_lo), y: 4, z: 8, core: 2. Of those that a mesh axis runs over, the one named last changes fastest.
Arguments:
- features: float32 [131072, 440], P(('row', 'col')), may hold values from -6 to 6
- targets: float32 [131072, 147], P(('row', 'col')), may hold values from -6 to 6
- block_ids: int32 [1, 2048], replicated, may hold values from 0 to 131071, as said below
Outputs:
- coefficients: float32 [131072, 147], P(('row', 'col'))
- residual: float32 [131072, 147], P(('row', 'col'))
The draws below stay inside these ranges and needn't reach their ends.
Inputs may be any that keep to these rules, and one draw needn't show every extreme that they name: In each row of block_ids the ids are distinct, and positions d * 8 to (d + 1) * 8 - 1 hold ids of examples d * 512 to (d + 1) * 512 - 1, for every d.
All inputs are finite; a program needn't handle non-finite values.
Results may differ from the reference program's by a relative error of at most 0.0003.
Values sent between devices are 32-bit elements; how exact they have to be, the bound alone decides.
No kernel may reach another device: no remote copies, remote signals or barrier semaphores. Data moves between devices by JAX's collectives and lax.ppermute only.
A program may use at most 128 MiB of HBM per device.

```python
import jax
import jax.numpy as jnp
from jax import lax

F = 440
C = 147
EX_DEV = 512
BLOCK_DEV = 8
STEPS = 1
BLOCK = 2048
N = 131072


def draw_block_ids(key, part):
    key = jax.random.fold_in(key, 7)
    owners = BLOCK // BLOCK_DEV
    keys = jax.random.split(key, STEPS * owners)
    perms = jax.vmap(lambda k: jax.random.permutation(k, EX_DEV))(keys)
    which = jnp.arange(STEPS * owners, dtype=jnp.int32)
    first = perms[:, 0]
    offset = jnp.where(which == 0, -first, jnp.where(which == owners - 1, EX_DEV - 1 - first, 0))
    picked = (perms[:, :BLOCK_DEV] + offset[:, None]) % EX_DEV
    base = which % owners * EX_DEV
    ids = picked + base[:, None]
    return ids.reshape(STEPS, BLOCK).astype(jnp.int32)


def block_levels(key, extent, shards, low, top_value):
    def one(position, parts):
        draws = jax.random.uniform(jax.random.fold_in(jax.random.fold_in(key, 6), position), (parts,), jnp.float32, low / len(shards), top_value / len(shards))
        return jnp.repeat(jnp.exp(draws), extent[position] // parts).reshape((-1,) + (1,) * (len(extent) - position - 1))

    loudness = one(*shards[0])
    for cut in shards[1:]:
        loudness = loudness * one(*cut)
    return loudness


def bell_draw(stream_key, dims, scale, most, cuts=(), held_as=jnp.bfloat16):
    drawn = scale * jax.random.normal(stream_key, dims, jnp.float32)
    if cuts:
        drawn = drawn * block_levels(stream_key, dims, cuts, -0.22, 0.18)
    return jnp.clip(drawn, -most, most).astype(held_as)


def setup_inputs(seed: int = 0) -> dict:
    key_list = jax.random.split(jax.random.key(seed), 4)
    features = bell_draw(key_list[0], (N, F), 1.0, 6.0, ((0, 256),), jnp.float32)
    targets = bell_draw(key_list[1], (N, C), 1.0, 6.0, ((0, 256),), jnp.float32)
    block_ids = draw_block_ids(jax.random.fold_in(key_list[3], 71), 0)
    return {"features": features, "targets": targets, "block_ids": block_ids}


RIDGE = 1.0

def kernel_tile(left, right):
    width = left.shape[1]
    left_sq = jnp.sum(left * left, axis=1)
    right_sq = jnp.sum(right * right, axis=1)
    inner = jnp.dot(left.astype(jnp.float32), right.T.astype(jnp.float32), precision=lax.Precision.HIGHEST, preferred_element_type=jnp.float32)
    return jnp.exp(-(left_sq[:, None] + right_sq[None, :] - 2.0 * inner) / width)

def tile_dot(left, right):
    return jnp.dot(left.astype(jnp.float32), right.astype(jnp.float32), precision=lax.Precision.HIGHEST, preferred_element_type=jnp.float32)

def block_solve(block_feat, block_res):
    gram = kernel_tile(block_feat, block_feat) + RIDGE * jnp.eye(block_feat.shape[0], dtype=jnp.float32)
    total = gram.shape[0]
    edge = min(512, total)
    count = total // edge
    lower = {}
    for j in range(count):
        for i in range(j, count):
            acc = gram[i * edge:(i + 1) * edge, j * edge:(j + 1) * edge]
            for k in range(j):
                acc = acc - tile_dot(lower[i, k], lower[j, k].T)
            if i == j:
                lower[j, j] = jnp.linalg.cholesky(acc)
            else:
                lower[i, j] = jax.scipy.linalg.solve_triangular(lower[j, j], acc.T, lower=True).T
    forward = []
    for i in range(count):
        acc = block_res[i * edge:(i + 1) * edge]
        for k in range(i):
            acc = acc - tile_dot(lower[i, k], forward[k])
        forward.append(jax.scipy.linalg.solve_triangular(lower[i, i], acc, lower=True))
    backward = [None] * count
    for i in range(count - 1, -1, -1):
        acc = forward[i]
        for k in range(i + 1, count):
            acc = acc - tile_dot(lower[k, i].T, backward[k])
        backward[i] = jax.scipy.linalg.solve_triangular(lower[i, i], acc, lower=True, trans=1)
    return jnp.concatenate(backward, axis=0)

def reference(features, targets, block_ids):
    coefficients = jnp.zeros_like(targets)
    residual = targets
    for step in range(STEPS):
        ids = block_ids[step]
        block_feat = features[ids]
        block_res = residual[ids]
        delta = block_solve(block_feat, block_res)
        groups = features.reshape(N // EX_DEV, EX_DEV, F)

        def apply_group(group):
            return jnp.dot(kernel_tile(group, block_feat).astype(jnp.float32), delta.astype(jnp.float32), precision=lax.Precision.HIGHEST, preferred_element_type=jnp.float32)
        update = lax.map(apply_group, groups).reshape(N, C)
        residual = residual - update
        residual = residual.at[ids].add(-RIDGE * delta)
        coefficients = coefficients.at[ids].add(delta)
    return (coefficients, residual)
```

```python
import functools
import jax
import jax.numpy as jnp
from jax import lax
from jax.experimental import pallas as pl
from jax.experimental.pallas import tpu as pltpu
from jax.sharding import PartitionSpec as P

BF, F32 = jnp.bfloat16, jnp.float32
T = 256
WIDE = 512


def split(x):
    hi = x.astype(BF)
    return hi, (x - hi.astype(F32)).astype(BF)


def left3(x):
    hi, lo = split(x)
    return jnp.concatenate([hi, lo, hi], axis=1)


def right3(x):
    hi, lo = split(x)
    return jnp.concatenate([hi, hi, lo], axis=0)


def mm(a, b):
    return jnp.dot(a, b, preferred_element_type=F32)


def mm_nt(a, b):
    return lax.dot_general(a, b, (((1,), (1,)), ((), ())), preferred_element_type=F32)


def eye_mask():
    return lax.broadcasted_iota(jnp.int32, (T, T), 0) == lax.broadcasted_iota(jnp.int32, (T, T), 1)


def inverse(block):
    eye = jnp.where(eye_mask(), 1.0, 0.0).astype(F32)
    low, high = 1.0, 1.0 + T
    delta = (high - low) / (high + low)
    c0 = 2.0 / (high + low)
    r = eye - c0 * block
    x = None
    for step in range(6):
        c = 2.0 / (2.0 - delta * delta)
        rr = right3(r)
        if step == 0:
            x_new = (c * c0) * (eye + r)
            sq = mm(left3(r), rr)
        elif step < 5:
            both = mm(jnp.concatenate([left3(r), left3(x)], axis=0), rr)
            sq = both[:T]
            x_new = c * (x + both[T:])
        else:
            sq = None
            x_new = c * (x + mm(left3(x), rr))
        if sq is not None:
            r = (1.0 - c) * eye + c * sq
        x = x_new
        delta = delta * delta / (2.0 - delta * delta)
    fix = eye - mm(left3(block), right3(x))
    return x + mm(left3(x), right3(fix))


def prep(f, width):
    lane = lax.broadcasted_iota(jnp.int32, f.shape, 1)
    f = jnp.where(lane < width, f, 0.0)
    half = -0.5 * jnp.sum(f * f, axis=1, keepdims=True)
    s1 = half.astype(BF).astype(F32)
    s2 = (half - s1).astype(BF).astype(F32)
    s3 = (half - s1 - s2).astype(BF).astype(F32)
    hi, lo = split(f)
    hi = hi.astype(F32)
    one = jnp.ones_like(half)
    a, b = hi, hi
    for n, (va, vb) in enumerate([(s1, one), (s2, one), (s3, one), (one, s1), (one, s2), (one, s3)]):
        at = lane == width + n
        a = jnp.where(at, va, a)
        b = jnp.where(at, vb, b)
    return a.astype(BF), b.astype(BF), lo


def kernel(width, classes, slots_ref, half_ref, other_ref, feat_ref, targ_ref, coef_ref, res_ref,
           s_ref, a_ref, b_ref, la_ref, t_ref, x_ref):
    n = 2 * half_ref.shape[0]
    nb = n // T
    rows = feat_ref.shape[0]
    scale = 2.0 / width
    off = half_ref.shape[1] - T

    def put(dst_a, dst_b, at, a, b, lo):
        if dst_a is not None:
            dst_a[at, 0:WIDE] = a
            dst_a[at, WIDE:2 * WIDE] = lo
            dst_a[at, 2 * WIDE:3 * WIDE] = a
        if dst_b is not None:
            dst_b[at, 0:WIDE] = b
            dst_b[at, WIDE:2 * WIDE] = b
            dst_b[at, 2 * WIDE:3 * WIDE] = lo

    for which, part in enumerate((half_ref, other_ref)):
        @pl.loop(0, nb // 2)
        def _(i):
            src = pl.ds(pl.multiple_of(i * T, T), T)
            at = pl.ds(pl.multiple_of(which * (n // 2) + i * T, T), T)
            a, b, lo = prep(part[src, 0:WIDE], width)
            put(a_ref, b_ref, at, a, b, lo)
            s_ref[at, n:n + T] = part[src, off:off + T]

    for i in range(rows // T):
        at = pl.ds(i * T, T)
        f = jnp.concatenate([feat_ref[at, :], jnp.zeros((T, WIDE - width), F32)], axis=1)
        a, b, lo = prep(f, width)
        put(la_ref, None, at, a, b, lo)

    for j in range(nb):
        k = jnp.exp(scale * mm_nt(a_ref[j * T:(j + 1) * T, :], b_ref[j * T:n, :]))
        s_ref[j * T:(j + 1) * T, j * T:(j + 1) * T] = jnp.where(eye_mask(), 2.0, k[:, :T])
        if j < nb - 1:
            s_ref[j * T:(j + 1) * T, (j + 1) * T:n] = k[:, T:]

    @pl.loop(0, nb)
    def _(i):
        at = pl.ds(pl.multiple_of(i * T, T), T)
        k = jnp.exp(scale * mm_nt(la_ref[...], b_ref[at, :]))
        hi, lo = split(k)
        t_ref[0, :, at] = hi
        t_ref[1, :, at] = lo

    for j in range(nb):
        here = slice(j * T, (j + 1) * T)
        rest = slice((j + 1) * T, n + T)
        w = inverse(s_ref[here, here])
        p = s_ref[here, rest]
        g = mm(left3(w), right3(p))
        s_ref[here, rest] = g
        g3 = right3(g)
        for i in range(j + 1, nb):
            lhs = left3(p[:, (i - j - 1) * T:(i - j) * T].T)
            s_ref[i * T:(i + 1) * T, i * T:n + T] -= mm(lhs, g3[:, (i - j - 1) * T:])

    for j in range(nb - 1, -1, -1):
        here = slice(j * T, (j + 1) * T)
        x = s_ref[here, n:n + T]
        if j < nb - 1:
            rest = slice((j + 1) * T, n)
            hi, lo = split(s_ref[here, rest])
            x = x - (mm(hi, x_ref[0, rest, :]) + mm(lo, x_ref[0, rest, :]) + mm(hi, x_ref[1, rest, :]))
        hi, lo = split(x)
        x_ref[0, here, :] = hi
        x_ref[1, here, :] = lo
    own = x[0:8, :]

    first = width - off
    upd = mm(t_ref[0], x_ref[0]) + mm(t_ref[1], x_ref[0]) + mm(t_ref[0], x_ref[1])
    upd = pltpu.roll(upd, T - first, 1)
    own = pltpu.roll(own, T - first, 1)
    res_ref[...] = targ_ref[...] - upd[:, :classes]
    coef_ref[...] = jnp.zeros_like(coef_ref)
    for i in range(8):
        at = pl.ds(slots_ref[i], 1)
        d = own[i:i + 1, :classes]
        coef_ref[at, :] = d
        res_ref[at, :] -= d


def solve_call(slots, half, other, feat, targ):
    width, classes = feat.shape[1], targ.shape[1]
    n = 2 * half.shape[0]
    rows = feat.shape[0]
    vm = pl.BlockSpec(memory_space=pltpu.VMEM)
    return pl.pallas_call(
        functools.partial(kernel, width, classes),
        out_shape=[jax.ShapeDtypeStruct(targ.shape, F32)] * 2,
        in_specs=[pl.BlockSpec(memory_space=pltpu.SMEM), vm, vm, vm, vm],
        out_specs=[vm, vm],
        scratch_shapes=[
            pltpu.VMEM((n, n + T), F32),
            pltpu.VMEM((n, 3 * WIDE), BF),
            pltpu.VMEM((n, 3 * WIDE), BF),
            pltpu.VMEM((rows, 3 * WIDE), BF),
            pltpu.VMEM((2, rows, n), BF),
            pltpu.VMEM((2, n, T), BF),
        ],
        compiler_params=pltpu.CompilerParams(vmem_limit_bytes=60 * 1024 * 1024),
        name="block_step",
    )(slots, half, other, feat, targ)


def place(x, y, z, core):
    return (((x % 2) * 4 + y) * 2 + core) * 16 + z * 2 + x // 2


def along(z_step=0, flip=0):
    return [
        (place(x, y, z, c), place(x, y, (z + z_step) % 8, c ^ flip))
        for x in range(4) for y in range(4) for z in range(8) for c in range(2)
    ]


def crossed(step, first):
    pairs = []
    for x in range(4):
        for y in range(4):
            for z in range(8):
                for c in range(2):
                    if (c == 0) == first:
                        to = place(x, (y + step) % 4, z, c)
                    else:
                        to = place((x + step) % 4, y, z, c)
                    pairs.append((place(x, y, z, c), to))
    return pairs


def send(a, pairs):
    return lax.ppermute(a, ("row", "col"), pairs)


def gather(a):
    rows = a.shape[0]
    near = jnp.concatenate([a, send(a, along(1)), send(a, along(7))], axis=0)
    a = jnp.concatenate([near, send(near, along(3)), send(near[: 2 * rows], along(5))], axis=0)
    for first in (True, False):
        a = jnp.concatenate([a] + [send(a, crossed(k, first)) for k in (1, 3, 2)], axis=0)
    return a, send(a, along(0, 1))


def per_device(features, targets, block_ids):
    ex_rows = features.shape[0]
    per_dev = block_ids.shape[1] // lax.axis_size(("row", "col"))
    me = lax.axis_index(("row", "col"))
    slots = lax.dynamic_slice_in_dim(block_ids, me * per_dev, per_dev, 1)[0] - me * ex_rows
    width = features.shape[1] + targets.shape[1]
    own = jnp.concatenate(
        [features[slots], targets[slots], jnp.zeros((per_dev, 640 - width), F32)], axis=1
    )
    half, other = gather(own)
    return tuple(solve_call(slots, half, other, features, targets))


def solution(mesh):
    spec = P(("row", "col"), None)
    return jax.shard_map(
        per_device, mesh=mesh, in_specs=(spec, spec, P()), out_specs=(spec, spec), check_vma=False
    )
```

```python
import functools

import jax
import jax.numpy as jnp
from jax import lax
from jax.experimental import pallas as pl
from jax.experimental.pallas import tpu as pltpu
from jax.sharding import PartitionSpec as P

BF, F32 = jnp.bfloat16, jnp.float32
T = 256
WIDE = 512
LANES = 640


def split(x):
    hi = x.astype(BF)
    return hi, (x - hi.astype(F32)).astype(BF)


def left3(x):
    hi, lo = split(x)
    return jnp.concatenate([hi, lo, hi], axis=1)


def right3(x):
    hi, lo = split(x)
    return jnp.concatenate([hi, hi, lo], axis=0)


def mm(a, b):
    return jnp.dot(a, b, preferred_element_type=F32)


def mm_nt(a, b, precision=None):
    return lax.dot_general(a, b, (((1,), (1,)), ((), ())), precision=precision, preferred_element_type=F32)


def iota(shape, dim):
    return lax.broadcasted_iota(jnp.int32, shape, dim)


def eye_mask():
    return iota((T, T), 0) == iota((T, T), 1)


def inverse(block):
    eye = jnp.where(eye_mask(), 1.0, 0.0).astype(F32)
    low, high = 1.0, 1.0 + T
    delta = (high - low) / (high + low)
    c0 = 2.0 / (high + low)
    r = eye - c0 * block
    x = None
    for step in range(6):
        c = 2.0 / (2.0 - delta * delta)
        sq = None
        if step == 0:
            sq = mm(left3(r), right3(r))
            yield
            x = (c * c0) * (eye + r)
        elif step < 5:
            both = mm(jnp.concatenate([left3(r), left3(x)], axis=0), right3(r))
            yield
            sq = both[:T]
            x = c * (x + both[T:])
        else:
            more = mm(x.astype(BF), r.astype(BF))
            yield
            x = c * (x + more)
        if sq is not None:
            r = (1.0 - c) * eye + c * sq
        delta = delta * delta / (2.0 - delta * delta)
    prod = mm(left3(block), right3(x))
    yield
    fix = eye - prod
    more = mm(x.astype(BF), fix.astype(BF))
    yield
    return x + more


NS_STEPS = 8


def run(chain, tasks):
    total = sum(cost for cost, _ in tasks)
    tasks = list(tasks)
    done, at = 0.0, 0
    while True:
        try:
            next(chain)
        except StopIteration as stop:
            for _, task in tasks:
                task()
            return stop.value
        at += 1
        while tasks and done < total * at / NS_STEPS:
            cost, task = tasks.pop(0)
            task()
            done += cost


def spare(half, one):
    s1 = half.astype(BF).astype(F32)
    s2 = (half - s1).astype(BF).astype(F32)
    s3 = (half - s1 - s2).astype(BF).astype(F32)
    return [(s1, one), (s2, one), (s3, one), (one, s1), (one, s2), (one, s3)]


def prep_rows(f, width):
    lane = iota(f.shape, 1)
    f = jnp.where(lane < width, f, 0.0)
    half = -0.5 * jnp.sum(f * f, axis=1, keepdims=True)
    hi, lo = split(f)
    a = b = hi.astype(F32)
    for n, (va, vb) in enumerate(spare(half, jnp.ones_like(half))):
        a = jnp.where(lane == width + n, va, a)
        b = jnp.where(lane == width + n, vb, b)
    return a.astype(BF), b.astype(BF), lo


def prep_local(ft, width):
    f = jnp.concatenate([ft, jnp.zeros((WIDE - width, ft.shape[1]), F32)], axis=0)
    row = iota(f.shape, 0)
    half = -0.5 * jnp.sum(f * f, axis=0, keepdims=True)
    hi, lo = split(f)
    a = hi.astype(F32)
    for n, (va, _) in enumerate(spare(half, jnp.ones_like(half))):
        a = jnp.where(row == width + n, va, a)
    return a.astype(BF), lo


def blk(i, count=1):
    return slice(i * T, (i + count) * T)


class Factor:
    def __init__(self, width, nb, refs, parts):
        self.width, self.nb, self.parts = width, nb, parts
        self.s, self.a, self.b, self.pt = refs
        self.w = {}

    def rows_of(self, i):
        for part in self.parts:
            count = part.shape[0] // T
            if i < count:
                return part, blk(i)
            i -= count
        raise IndexError(i)

    def prep(self, i):
        part, at = self.rows_of(i)
        a, b, lo = prep_rows(part[at, 0:WIDE], self.width)
        for ref, hi in ((self.a, a), (self.b, b)):
            ref[blk(i), 0:WIDE] = hi
            ref[blk(i), WIDE:] = lo

    def gram(self, k):
        if k == self.nb:
            for i in range(self.nb):
                part, at = self.rows_of(i)
                self.s[blk(i), blk(k)] = part[at, LANES - T:]
            return
        left = self.a[0:(k + 1) * T, :]
        left = jnp.concatenate([left, left[:, :WIDE]], axis=1)
        b = self.b[blk(k), :]
        right = jnp.concatenate([b[:, :WIDE], b], axis=1)
        g = jnp.exp((2.0 / self.width) * mm_nt(left, right))
        if k:
            self.s[0:k * T, blk(k)] = g[:k * T]
        self.s[blk(k), blk(k)] = jnp.where(eye_mask(), 2.0, g[k * T:])

    def column(self, j, k):
        p = self.s[blk(j), blk(k)]
        last = min(k, self.nb - 1)
        if k < self.nb:
            self.pt[blk(k), :] = left3(p.T)
        g = mm(left3(self.w[j]), right3(p))
        self.s[blk(j), blk(k)] = g
        if last > j:
            self.s[blk(j + 1, last - j), blk(k)] -= mm(self.pt[blk(j + 1, last - j), :], right3(g))

    def task_column(self, j, k):
        return (1 + min(k, self.nb - 1) - j, functools.partial(self.column, j, k))

    def task_gram(self, k):
        return (2.2 * (k + 1) if k < self.nb else 0.5, functools.partial(self.gram, k))

    def go(self, known, columns, extra):
        m = len(known)
        self.w = dict(enumerate(known))
        for k in range(m + 1):
            self.prep(k)
            self.gram(k)
            for j in range(k):
                self.column(j, k)
        for j in range(m, self.nb):
            tasks = []
            for k in range(j + 1, columns):
                if j == m:
                    if k < self.nb:
                        tasks.append((0.7, functools.partial(self.prep, k)))
                    tasks.append(self.task_gram(k))
                    tasks += [self.task_column(i, k) for i in range(m)]
                else:
                    tasks.append(self.task_column(j - 1, k))
            tasks += extra.get(j, [])
            self.w[j] = run(inverse(self.s[blk(j), blk(j)]), tasks)
            if j + 1 < columns:
                self.column(j, j + 1)


def scratch_for(nb, cols):
    return [
        pltpu.VMEM((nb * T, cols * T), F32),
        pltpu.VMEM((nb * T, 2 * WIDE), BF),
        pltpu.VMEM((nb * T, 2 * WIDE), BF),
        pltpu.VMEM((nb * T, 3 * T), BF),
    ]


VM = pl.BlockSpec(memory_space=pltpu.VMEM)
SM = pl.BlockSpec(memory_space=pltpu.SMEM)


def onehot(ids_ref, me, per_dev, rows):
    row, lane = iota((per_dev, rows), 0), iota((per_dev, rows), 1)
    hot = jnp.zeros((per_dev, rows), F32)
    for i in range(per_dev):
        slot = ids_ref[0, me * per_dev + i] - me * rows
        hot = jnp.where((row == i) & (lane == slot), 1.0, hot)
    return hot


def own_kernel(per_dev, ids_ref, me_ref, feat_ref, targ_ref, out_ref):
    hot = onehot(ids_ref, me_ref[0], per_dev, feat_ref.shape[1])
    top = jnp.concatenate(
        [feat_ref[...], targ_ref[...],
         jnp.zeros((LANES - feat_ref.shape[0] - targ_ref.shape[0], feat_ref.shape[1]), F32)], axis=0)
    out_ref[...] = mm_nt(hot, top, lax.Precision.HIGHEST)


def own_rows(ids, me, feat_t, targ_t, per_dev):
    return pl.pallas_call(
        functools.partial(own_kernel, per_dev),
        out_shape=jax.ShapeDtypeStruct((per_dev, LANES), F32),
        in_specs=[SM, SM, VM, VM],
        out_specs=VM,
        name="own_rows",
    )(ids, me, feat_t, targ_t)


def step_kernel(per_dev, n_parts, n_known, ids_ref, me_ref, feat_ref, targ_ref, *refs):
    parts, refs = refs[:n_parts], refs[n_parts:]
    known = [refs[0][blk(i), :] for i in range(n_known)] if n_known else []
    refs = refs[1:] if n_known else refs
    coef_ref, res_ref, t_ref, la_ref = refs[:4]
    scratch = refs[4:]
    width, rows = feat_ref.shape
    classes = targ_ref.shape[0]
    nb = sum(p.shape[0] for p in parts) // T
    fac = Factor(width, nb, scratch, parts)

    a, lo = prep_local(feat_ref[...], width)
    la_ref[0:WIDE, :] = a
    la_ref[WIDE:, :] = lo

    def tile(i):
        b = fac.b[blk(i), :]
        left = jnp.concatenate([b, b[:, :WIDE]], axis=1)
        right = jnp.concatenate([la_ref[0:WIDE, :], la_ref[...]], axis=0)
        hi, lo = split(jnp.exp((2.0 / width) * mm(left, right)))
        t_ref[0, blk(i), :] = hi
        t_ref[1, blk(i), :] = lo

    extra = {}
    per_slot = {0: (0, 0, 0, 0, 1, 2, 2, 3)}.get(n_known, (0, 0, 0, 0, 0, 2, 3, 3))
    at = 0
    for j, count in enumerate(per_slot):
        extra[j] = [(5.0, functools.partial(tile, at + i)) for i in range(count)]
        at += count
    fac.go(known, nb + 1, extra)

    upd = jnp.zeros((T, rows), F32)
    rhs = blk(nb)
    for k in range(nb - 1, -1, -1):
        x = fac.s[blk(k), rhs]
        x3 = right3(x)
        if k:
            fac.s[blk(k - 1), rhs] -= mm(left3(fac.s[blk(k - 1), blk(k)]), x3)
        if k > 1:
            fac.s[0:(k - 1) * T, rhs] -= mm(left3(fac.s[0:(k - 1) * T, blk(k)]), x3)
        t3 = jnp.concatenate([t_ref[0, blk(k), :], t_ref[0, blk(k), :], t_ref[1, blk(k), :]], axis=0)
        upd = upd + mm(left3(x.T), t3)

    first = width - (LANES - T)
    hot = onehot(ids_ref, me_ref[0], per_dev, rows)
    own = lax.dot_general(x[0:per_dev, :], hot, (((0,), (0,)), ((), ())),
                          precision=lax.Precision.HIGHEST, preferred_element_type=F32)
    coef_ref[...] = own[first:first + classes, :]
    res_ref[...] = targ_ref[...] - upd[first:first + classes, :] - own[first:first + classes, :]


def solve_call(ids, me, feat_t, targ_t, parts, known, per_dev):
    nb = sum(p.shape[0] for p in parts) // T
    rows = feat_t.shape[1]
    n_known = known.shape[0] // T if known is not None else 0
    args = [ids, me, feat_t, targ_t] + list(parts) + ([known] if n_known else [])
    return pl.pallas_call(
        functools.partial(step_kernel, per_dev, len(parts), n_known),
        out_shape=[jax.ShapeDtypeStruct(targ_t.shape, F32)] * 2,
        in_specs=[SM, SM] + [VM] * (len(args) - 2),
        out_specs=[VM, VM],
        scratch_shapes=[pltpu.VMEM((2, nb * T, rows), BF), pltpu.VMEM((2 * WIDE, rows), BF)]
        + scratch_for(nb, nb + 1),
        compiler_params=pltpu.CompilerParams(vmem_limit_bytes=58 * 1024 * 1024),
        name="block_step",
    )(*args)


def place(x, y, z, core):
    return (((x % 2) * 4 + y) * 2 + core) * 16 + z * 2 + x // 2


def along(z_step=0, flip=0):
    return [
        (place(x, y, z, c), place(x, y, (z + z_step) % 8, c ^ flip))
        for x in range(4) for y in range(4) for z in range(8) for c in range(2)
    ]


def crossed(step, first):
    pairs = []
    for x in range(4):
        for y in range(4):
            for z in range(8):
                for c in range(2):
                    if (c == 0) == first:
                        to = place(x, (y + step) % 4, z, c)
                    else:
                        to = place((x + step) % 4, y, z, c)
                    pairs.append((place(x, y, z, c), to))
    return pairs


def send(a, pairs):
    return lax.ppermute(a, ("row", "col"), pairs)


def gather(a):
    rows = a.shape[0]
    near = jnp.concatenate([a, send(a, along(1)), send(a, along(7))], axis=0)
    a = jnp.concatenate([near, send(near, along(3)), send(near[: 2 * rows], along(5))], axis=0)
    for first in (True, False):
        a = jnp.concatenate([a] + [send(a, crossed(k, first)) for k in (1, 3, 2)], axis=0)
    return a, send(a, along(0, 1))


def per_device(features, targets, block_ids):
    per_dev = block_ids.shape[1] // lax.axis_size(("row", "col"))
    me = jnp.reshape(lax.axis_index(("row", "col")), (1,))
    feat_t, targ_t = features.T, targets.T
    parts = gather(own_rows(block_ids, me, feat_t, targ_t, per_dev))
    coef_t, res_t = solve_call(block_ids, me, feat_t, targ_t, parts, None, per_dev)
    return coef_t.T, res_t.T


def solution(mesh):
    spec = P(("row", "col"), None)
    return jax.shard_map(
        per_device, mesh=mesh, in_specs=(spec, spec, P()), out_specs=(spec, spec), check_vma=False
    )
```

```python
import functools

import jax
import jax.numpy as jnp
from jax import lax
from jax.experimental import pallas as pl
from jax.experimental.pallas import tpu as pltpu
from jax.sharding import PartitionSpec as P

BF, F32 = jnp.bfloat16, jnp.float32
T = 256
WIDE = 512
LANES = 640
RHS_AT, RHS = 48, 160


def split(x):
    hi = x.astype(BF)
    return hi, (x - hi.astype(F32)).astype(BF)


def left3(x):
    hi, lo = split(x)
    return jnp.concatenate([hi, lo, hi], axis=1)


def right3(x):
    hi, lo = split(x)
    return jnp.concatenate([hi, hi, lo], axis=0)


def mm(a, b):
    return jnp.dot(a, b, preferred_element_type=F32)


def mm_nt(a, b, precision=None):
    return lax.dot_general(a, b, (((1,), (1,)), ((), ())), precision=precision, preferred_element_type=F32)


def iota(shape, dim):
    return lax.broadcasted_iota(jnp.int32, shape, dim)


def eye_mask():
    return iota((T, T), 0) == iota((T, T), 1)


def rates(kappa, steps):
    delta = (kappa - 1.0) / (kappa + 1.0)
    out = []
    for _ in range(steps):
        out.append(2.0 / (2.0 - delta * delta))
        delta = delta * delta / (2.0 - delta * delta)
    return 2.0 / (1.0 + kappa), out, (1.0 + delta) / (1.0 - delta)


def eye():
    return jnp.where(eye_mask(), 1.0, 0.0).astype(F32)


def start(block, x_ref, r_ref):
    first, factors, kappa = rates(1.0 + T, 2)
    late = 2.0 / (1.0 + kappa)
    x_ref[...] = late * eye()
    r_ref[...] = eye() - late * block
    top = jnp.max(jnp.sum(jnp.abs(block), axis=1, keepdims=True))

    @pl.when(jnp.logical_not(top <= kappa))
    def _():
        r = eye() - first * block
        x = (factors[0] * first) * (eye() + r)
        r = (1.0 - factors[0]) * eye() + factors[0] * mm(left3(r), right3(r))
        rr = right3(r)
        x_ref[...] = factors[1] * (x + mm(left3(x), rr))
        r_ref[...] = (1.0 - factors[1]) * eye() + factors[1] * mm(left3(r), rr)

    return kappa


def inverse(block, x_ref, r_ref, kappa):
    _, factors, _ = rates(kappa, 4)
    x, r = x_ref[...], r_ref[...]
    for step, c in enumerate(factors):
        if step == 2:
            rb = r.astype(BF)
            sq, more = mm(rb, rb), mm(x.astype(BF), rb)
            yield
            x = c * (x + more)
            r = (1.0 - c) * eye() + c * sq
        elif step < 3:
            rr = right3(r)
            sq = mm(left3(r), rr)
            more = mm(left3(x), rr)
            yield
            x = c * (x + more)
            r = (1.0 - c) * eye() + c * sq
        else:
            more = mm(x.astype(BF), r.astype(BF))
            yield
            x = c * (x + more)
    prod = mm(left3(block), right3(x))
    yield
    fix = eye() - prod
    more = mm(x.astype(BF), fix.astype(BF))
    yield
    return x + more


NS_STEPS = 6


def run(chain, tasks):
    total = sum(cost for cost, _ in tasks)
    tasks = list(tasks)
    done, at = 0.0, 0
    while True:
        try:
            next(chain)
        except StopIteration as stop:
            for _, task in tasks:
                task()
            return stop.value
        at += 1
        while tasks and done < total * at / NS_STEPS:
            cost, task = tasks.pop(0)
            task()
            done += cost


def spare(half, one):
    s1 = half.astype(BF).astype(F32)
    s2 = (half - s1).astype(BF).astype(F32)
    s3 = (half - s1 - s2).astype(BF).astype(F32)
    return [(s1, one), (s2, one), (s3, one), (one, s1), (one, s2), (one, s3)]


def prep_rows(f, width):
    base = width // 128 * 128
    main, tail = f[:, :base], f[:, base:]
    lane = iota(tail.shape, 1) + base
    tail = jnp.where(lane < width, tail, 0.0)
    half = -0.5 * (jnp.sum(main * main, axis=1, keepdims=True) + jnp.sum(tail * tail, axis=1, keepdims=True))
    hi, lo = split(main)
    tail_hi, tail_lo = split(tail)
    a = b = tail_hi.astype(F32)
    for n, (va, vb) in enumerate(spare(half, jnp.ones_like(half))):
        a = jnp.where(lane == width + n, va, a)
        b = jnp.where(lane == width + n, vb, b)
    join = lambda p, q: jnp.concatenate([p, q], axis=1)
    return join(hi, a.astype(BF)), join(hi, b.astype(BF)), join(lo, tail_lo)


def prep_local(ft, width):
    f = jnp.concatenate([ft, jnp.zeros((WIDE - width, ft.shape[1]), F32)], axis=0)
    row = iota(f.shape, 0)
    half = -0.5 * jnp.sum(f * f, axis=0, keepdims=True)
    hi, lo = split(f)
    a = hi.astype(F32)
    for n, (va, _) in enumerate(spare(half, jnp.ones_like(half))):
        a = jnp.where(row == width + n, va, a)
    return a.astype(BF), lo


def blk(i, count=1):
    return slice(i * T, (i + count) * T)


class Factor:
    def __init__(self, width, nb, refs, parts, rhs=True):
        self.width, self.nb, self.parts, self.rhs = width, nb, parts, rhs
        self.s, self.a, self.b, self.q, self.g, self.x, self.r = refs
        self.bottom = nb + 1 if rhs else nb

    def at(self, first, count):
        stop = (first + count) * T
        return slice(first * T, self.nb * T + RHS if stop > self.nb * T else stop)

    def rows_of(self, i):
        for part in self.parts:
            count = part.shape[0] // T
            if i < count:
                return part, blk(i)
            i -= count
        raise IndexError(i)

    def prep(self, i):
        part, at = self.rows_of(i)
        a, b, lo = prep_rows(part[at, 0:WIDE], self.width)
        for ref, hi in ((self.a, a), (self.b, b)):
            ref[blk(i), 0:WIDE] = hi
            ref[blk(i), WIDE:] = lo
        if self.rhs:
            self.s[blk(self.nb).start:, blk(i)] = part[at, LANES - T:].T[RHS_AT:RHS_AT + RHS]

    def gram(self, i, first, count):
        left = self.a[blk(first, count), :]
        left = jnp.concatenate([left, left[:, :WIDE]], axis=1)
        b = self.b[blk(i), :]
        right = jnp.concatenate([b[:, :WIDE], b], axis=1)
        g = jnp.exp((2.0 / self.width) * mm_nt(left, right))
        if first == i:
            self.s[blk(i), blk(i)] = jnp.where(eye_mask(), 2.0, g[:T])
            first, count, g = first + 1, count - 1, g[T:]
        if count:
            self.s[blk(first, count), blk(i)] = g

    def split_column(self, j, i):
        hi, lo = split(self.s[self.at(i, 1), blk(j)])
        self.q[self.at(i, 1), 0:T] = hi
        self.q[self.at(i, 1), T:] = lo

    def q3(self, first, count):
        q = self.q[self.at(first, count), :]
        return jnp.concatenate([q, q[:, :T]], axis=1)

    def scale(self, w3, j, i):
        g = mm(self.q3(i, 1), w3)
        hi, lo = split(g)
        self.g[self.at(i, 1), 0:T] = hi
        self.g[self.at(i, 1), T:] = lo
        self.s[self.at(i, 1), blk(j)] = g

    def update(self, i, first, count):
        g = self.g[blk(i), :]
        right = jnp.concatenate([g[:, :T], g], axis=1)
        self.s[self.at(first, count), blk(i)] -= mm_nt(self.q3(first, count), right)

    def go(self, known, extra):
        nb, bottom = self.nb, self.bottom
        call = functools.partial
        self.prep(0)
        self.gram(0, 0, 1)
        tasks = []
        for i in range(1, nb):
            tasks.append((0.6, call(self.prep, i)))
        if nb > 1:
            tasks.append((2.0 * (nb - 1), call(self.gram, 0, 1, nb - 1)))
        for i in range(1, nb):
            tasks.append((2.0 * (nb - i), call(self.gram, i, i, nb - i)))
        self.w = dict(known)
        for j in range(nb):
            for i in range(j + 1, bottom):
                tasks.append((0.2, call(self.split_column, j, i)))
            tasks += extra.get(j, [])
            if j in self.w:
                for _, task in tasks:
                    task()
            else:
                block = self.s[blk(j), blk(j)]
                kappa = start(block, self.x, self.r)
                self.w[j] = run(inverse(block, self.x, self.r, kappa), tasks)
            tasks = []
            w3 = right3(self.w[j])
            if j + 1 < nb:
                self.scale(w3, j, j + 1)
                self.update(j + 1, j + 1, 1)
                for i in range(j + 2, bottom):
                    tasks.append((1.2, call(self.scale, w3, j, i)))
                for i in range(j + 1, nb):
                    first = max(i, j + 2)
                    if first < bottom:
                        tasks.append((bottom - first, call(self.update, i, first, bottom - first)))
            elif self.rhs:
                self.scale(w3, j, nb)


def scratch_for(nb, rhs):
    rows = nb * T + rhs
    return [
        pltpu.VMEM((rows, nb * T), F32),
        pltpu.VMEM((nb * T, 2 * WIDE), BF),
        pltpu.VMEM((nb * T, 2 * WIDE), BF),
        pltpu.VMEM((rows, 2 * T), BF),
        pltpu.VMEM((rows, 2 * T), BF),
        pltpu.VMEM((T, T), F32),
        pltpu.VMEM((T, T), F32),
    ]


def local(feat_ref, la_ref):
    a, lo = prep_local(feat_ref[...], feat_ref.shape[0])
    la_ref[0:WIDE, :] = a
    la_ref[WIDE:, :] = lo


def tile(fac, la_ref, t_ref, i, to):
    b = fac.b[blk(i), :]
    left = jnp.concatenate([b, b[:, :WIDE]], axis=1)
    right = jnp.concatenate([la_ref[0:WIDE, :], la_ref[...]], axis=0)
    hi, lo = split(jnp.exp((2.0 / fac.width) * mm(left, right)))
    t_ref[0, blk(to), :] = hi
    t_ref[1, blk(to), :] = lo


VM = pl.BlockSpec(memory_space=pltpu.VMEM)
SM = pl.BlockSpec(memory_space=pltpu.SMEM)


def onehot(ids_ref, me, per_dev, rows):
    row, lane = iota((per_dev, rows), 0), iota((per_dev, rows), 1)
    hot = jnp.zeros((per_dev, rows), F32)
    for i in range(per_dev):
        slot = ids_ref[0, me * per_dev + i] - me * rows
        hot = jnp.where((row == i) & (lane == slot), 1.0, hot)
    return hot


def own_kernel(per_dev, ids_ref, me_ref, feat_ref, targ_ref, out_ref):
    rows = feat_ref.shape[1]
    hot = onehot(ids_ref, me_ref[0], per_dev, rows)
    hot = jnp.concatenate([hot, jnp.zeros((128 - per_dev, rows), F32)], axis=0).astype(BF)
    both = jnp.concatenate(
        [feat_ref[...], targ_ref[...],
         jnp.zeros((LANES - feat_ref.shape[0] - targ_ref.shape[0], rows), F32)], axis=0)
    hi = both.astype(BF)
    rest = both - hi.astype(F32)
    mid = rest.astype(BF)
    low = (rest - mid.astype(F32)).astype(BF)
    picked = mm_nt(hi, hot) + mm_nt(mid, hot) + mm_nt(low, hot)
    out_ref[...] = picked.T[0:per_dev, :]


def own_rows(ids, me, feat_t, targ_t, per_dev):
    return pl.pallas_call(
        functools.partial(own_kernel, per_dev),
        out_shape=jax.ShapeDtypeStruct((per_dev, LANES), F32),
        in_specs=[SM, SM, VM, VM],
        out_specs=VM,
        name="own_rows",
    )(ids, me, feat_t, targ_t)


def step_kernel(per_dev, n_parts, has, ids_ref, me_ref, feat_ref, targ_ref, *refs):
    parts, refs = refs[:n_parts], refs[n_parts:]
    known, m = {}, 0
    if has:
        w_ref, la_ref, early_ref, refs = refs[0], refs[1], refs[2], refs[3:]
        m = w_ref.shape[0] // T
        known = {i: w_ref[blk(i), :] for i in range(m)}
    coef_ref, res_ref, t_ref = refs[:3]
    refs = refs[3:]
    if not has:
        la_ref, refs = refs[0], refs[1:]
    width, rows = feat_ref.shape
    classes = targ_ref.shape[0]
    nb = sum(p.shape[0] for p in parts) // T
    fac = Factor(width, nb, refs, parts)

    extra, at = {}, m
    for j, count in enumerate((0, 0, 0, 0, 0, 2, 3, 3) if m == 0 else (0, 0, 0, 0, 0, 1, 2, 3) if m == 2 else (0, 0, 0, 0, 0, 2, 2, 3)):
        extra[j] = [(5.0, functools.partial(tile, fac, la_ref, t_ref, at + i, at + i - m)) for i in range(count)]
        at += count
    if not has:
        extra[4] = [(2.0, functools.partial(local, feat_ref, la_ref))]
    fac.go(known, extra)

    upd = jnp.zeros((RHS, rows), F32)
    s = fac.s
    low = fac.at(nb, 1)
    for k in range(nb - 1, -1, -1):
        x = s[low, blk(k)]
        x3 = left3(x)
        if k:
            s[low, blk(k - 1)] -= mm(x3, right3(s[blk(k), blk(k - 1)]))
        if k > 1:
            s[low, 0:(k - 1) * T] -= mm(x3, right3(s[blk(k), 0:(k - 1) * T]))
        ref, at = (early_ref, blk(k)) if k < m else (t_ref, blk(k - m))
        t3 = jnp.concatenate([ref[0, at, :], ref[0, at, :], ref[1, at, :]], axis=0)
        upd = upd + mm(x3, t3)

    first = width - (LANES - T) - RHS_AT
    hot = onehot(ids_ref, me_ref[0], per_dev, rows)
    hot = jnp.concatenate([hot, jnp.zeros((128 - per_dev, rows), F32)], axis=0)
    own = jnp.dot(x[:, 0:128], hot, precision=lax.Precision.HIGHEST, preferred_element_type=F32)
    own = own[first:first + classes]
    coef_ref[...] = own
    res_ref[...] = targ_ref[...] - upd[first:first + classes, :] - own


def solve_call(ids, me, feat_t, targ_t, parts, given, per_dev):
    nb = sum(p.shape[0] for p in parts) // T
    rows = feat_t.shape[1]
    given = list(given) if given else []
    m = given[0].shape[0] // T if given else 0
    args = [ids, me, feat_t, targ_t] + list(parts) + given
    extra = [] if given else [pltpu.VMEM((2 * WIDE, rows), BF)]
    return pl.pallas_call(
        functools.partial(step_kernel, per_dev, len(parts), bool(given)),
        out_shape=[jax.ShapeDtypeStruct(targ_t.shape, F32)] * 2,
        in_specs=[SM, SM] + [VM] * (len(args) - 2),
        out_specs=[VM, VM],
        scratch_shapes=[pltpu.VMEM((2, (nb - m) * T, rows), BF)] + extra + scratch_for(nb, RHS),
        compiler_params=pltpu.CompilerParams(vmem_limit_bytes=58 * 1024 * 1024),
        name="block_step",
    )(*args)


def place(x, y, z, core):
    return (((x % 2) * 4 + y) * 2 + core) * 16 + z * 2 + x // 2


def along(z_step=0, flip=0):
    return [
        (place(x, y, z, c), place(x, y, (z + z_step) % 8, c ^ flip))
        for x in range(4) for y in range(4) for z in range(8) for c in range(2)
    ]


def crossed(step, first):
    pairs = []
    for x in range(4):
        for y in range(4):
            for z in range(8):
                for c in range(2):
                    if (c == 0) == first:
                        to = place(x, (y + step) % 4, z, c)
                    else:
                        to = place((x + step) % 4, y, z, c)
                    pairs.append((place(x, y, z, c), to))
    return pairs


def send(a, pairs):
    return lax.ppermute(a, ("row", "col"), pairs)


def per_device(features, targets, block_ids):
    per_dev = block_ids.shape[1] // lax.axis_size(("row", "col"))
    me = jnp.reshape(lax.axis_index(("row", "col")), (1,))
    feat_t, targ_t = features.T, targets.T
    own = own_rows(block_ids, me, feat_t, targ_t, per_dev)
    near = jnp.concatenate([own, send(own, along(1)), send(own, along(7))], axis=0)
    line = jnp.concatenate([near, send(near, along(3)), send(near, along(5))[: 2 * per_dev]], axis=0)
    plane = jnp.concatenate([line] + [send(line, crossed(k, True)) for k in (1, 3, 2)], axis=0)
    twin = send(plane, along(0, 1))
    sides = [send(plane, crossed(k, False)) for k in (1, 3, 2)]
    twins = [send(side, along(0, 1)) for side in sides]
    parts = [plane, twin] + sides[:2] + twins[:2] + sides[2:] + twins[2:]
    coef_t, res_t = solve_call(block_ids, me, feat_t, targ_t, parts, None, per_dev)
    return coef_t.T, res_t.T


def solution(mesh):
    spec = P(("row", "col"), None)
    return jax.shard_map(
        per_device, mesh=mesh, in_specs=(spec, spec, P()), out_specs=(spec, spec), check_vma=False
    )
```

```python
import functools

import jax
import jax.numpy as jnp
from jax import lax
from jax.experimental import pallas as pl
from jax.experimental.pallas import tpu as pltpu
from jax.sharding import PartitionSpec as P

BF, F32 = jnp.bfloat16, jnp.float32
T = 256
WIDE = 512
LANES = 640
RHS_AT, RHS = 48, 160


def split(x):
    hi = x.astype(BF)
    return hi, (x - hi.astype(F32)).astype(BF)


def left3(x):
    hi, lo = split(x)
    return jnp.concatenate([hi, lo, hi], axis=1)


def right3(x):
    hi, lo = split(x)
    return jnp.concatenate([hi, hi, lo], axis=0)


def mm(a, b):
    return jnp.dot(a, b, preferred_element_type=F32)


def mm_nt(a, b, precision=None):
    return lax.dot_general(a, b, (((1,), (1,)), ((), ())), precision=precision, preferred_element_type=F32)


def iota(shape, dim):
    return lax.broadcasted_iota(jnp.int32, shape, dim)


def eye_mask():
    return iota((T, T), 0) == iota((T, T), 1)


def inverse(block):
    eye = jnp.where(eye_mask(), 1.0, 0.0).astype(F32)
    low, high = 1.0, 1.0 + T
    delta = (high - low) / (high + low)
    c0 = 2.0 / (high + low)
    r = eye - c0 * block
    x = None
    for step in range(6):
        c = 2.0 / (2.0 - delta * delta)
        if step == 4:
            rb = r.astype(BF)
            sq, more = mm(rb, rb), mm(x.astype(BF), rb)
            yield
            x = c * (x + more)
            r = (1.0 - c) * eye + c * sq
        elif step < 5:
            rr = right3(r)
            sq = mm(left3(r), rr)
            more = None if x is None else mm(left3(x), rr)
            yield
            x = (c * c0) * (eye + r) if x is None else c * (x + more)
            r = (1.0 - c) * eye + c * sq
        else:
            more = mm(x.astype(BF), r.astype(BF))
            yield
            x = c * (x + more)
        delta = delta * delta / (2.0 - delta * delta)
    prod = mm(left3(block), right3(x))
    yield
    fix = eye - prod
    more = mm(x.astype(BF), fix.astype(BF))
    yield
    return x + more


SLOTS = 10


def run(chain, tasks):
    total = sum(cost for cost, _ in tasks)
    tasks = list(tasks)
    done, at = 0.0, 0
    while True:
        try:
            next(chain)
        except StopIteration as stop:
            for _, task in tasks:
                task()
            return stop.value
        at += 1
        while tasks and done < total * at / SLOTS:
            cost, task = tasks.pop(0)
            task()
            done += cost


def spare(half, one):
    s1 = half.astype(BF).astype(F32)
    s2 = (half - s1).astype(BF).astype(F32)
    s3 = (half - s1 - s2).astype(BF).astype(F32)
    return [(s1, one), (s2, one), (s3, one), (one, s1), (one, s2), (one, s3)]


def prep_rows(f, width):
    base = width // 128 * 128
    main, tail = f[:, :base], f[:, base:]
    lane = iota(tail.shape, 1) + base
    tail = jnp.where(lane < width, tail, 0.0)
    half = -0.5 * (jnp.sum(main * main, axis=1, keepdims=True) + jnp.sum(tail * tail, axis=1, keepdims=True))
    hi, lo = split(main)
    tail_hi, tail_lo = split(tail)
    a = b = tail_hi.astype(F32)
    for n, (va, vb) in enumerate(spare(half, jnp.ones_like(half))):
        a = jnp.where(lane == width + n, va, a)
        b = jnp.where(lane == width + n, vb, b)
    join = lambda p, q: jnp.concatenate([p, q], axis=1)
    return join(hi, a.astype(BF)), join(hi, b.astype(BF)), join(lo, tail_lo)


def prep_local(ft, width):
    f = jnp.concatenate([ft, jnp.zeros((WIDE - width, ft.shape[1]), F32)], axis=0)
    row = iota(f.shape, 0)
    half = -0.5 * jnp.sum(f * f, axis=0, keepdims=True)
    hi, lo = split(f)
    a = hi.astype(F32)
    for n, (va, _) in enumerate(spare(half, jnp.ones_like(half))):
        a = jnp.where(row == width + n, va, a)
    return a.astype(BF), lo


def blk(i, count=1):
    return slice(i * T, (i + count) * T)


class Factor:
    def __init__(self, width, nb, refs, parts):
        self.width, self.nb, self.parts = width, nb, parts
        self.s, self.a, self.b, self.q, self.g = refs

    def at(self, first, count):
        stop = (first + count) * T
        return slice(first * T, self.nb * T + RHS if stop > self.nb * T else stop)

    def rows_of(self, i):
        for part in self.parts:
            count = part.shape[0] // T
            if i < count:
                return part, blk(i)
            i -= count
        raise IndexError(i)

    def prep(self, i):
        part, at = self.rows_of(i)
        a, b, lo = prep_rows(part[at, 0:WIDE], self.width)
        for ref, hi in ((self.a, a), (self.b, b)):
            ref[blk(i), 0:WIDE] = hi
            ref[blk(i), WIDE:] = lo
        self.s[self.nb * T:, blk(i)] = part[at, LANES - T:].T[RHS_AT:RHS_AT + RHS]

    def gram(self, i, first, count):
        left = self.a[blk(first, count), :]
        left = jnp.concatenate([left, left[:, :WIDE]], axis=1)
        b = self.b[blk(i), :]
        right = jnp.concatenate([b[:, :WIDE], b], axis=1)
        g = jnp.exp((2.0 / self.width) * mm_nt(left, right))
        if first == i:
            self.s[blk(i), blk(i)] = jnp.where(eye_mask(), 2.0, g[:T])
            first, count, g = first + 1, count - 1, g[T:]
        if count:
            self.s[blk(first, count), blk(i)] = g

    def split_column(self, j, i):
        hi, lo = split(self.s[self.at(i, 1), blk(j)])
        self.q[self.at(i, 1), 0:T] = hi
        self.q[self.at(i, 1), T:] = lo

    def q3(self, first, count):
        q = self.q[self.at(first, count), :]
        return jnp.concatenate([q, q[:, :T]], axis=1)

    def scale(self, w3, j, i):
        g = mm(self.q3(i, 1), w3)
        hi, lo = split(g)
        self.g[self.at(i, 1), 0:T] = hi
        self.g[self.at(i, 1), T:] = lo
        self.s[self.at(i, 1), blk(j)] = g

    def update(self, i, first, count):
        g = self.g[blk(i), :]
        right = jnp.concatenate([g[:, :T], g], axis=1)
        self.s[self.at(first, count), blk(i)] -= mm_nt(self.q3(first, count), right)

    def chain(self, j, w3):
        if j:
            self.scale(w3, j - 1, j)
            yield
            self.update(j, j, 1)
            yield
        else:
            self.prep(0)
            yield
            self.gram(0, 0, 1)
            yield
        block = self.s[blk(j), blk(j)]
        w = yield from inverse(block)
        return w

    def go(self, extra):
        nb, bottom = self.nb, self.nb + 1
        call = functools.partial
        w3 = None
        for j in range(nb):
            tasks = []
            if j == 0:
                for i in range(1, nb):
                    tasks.append((0.6, call(self.prep, i)))
                tasks.append((2.0 * (nb - 1), call(self.gram, 0, 1, nb - 1)))
                for i in range(1, nb):
                    tasks.append((2.0 * (nb - i), call(self.gram, i, i, nb - i)))
            else:
                for i in range(j + 1, bottom):
                    tasks.append((1.2, call(self.scale, w3, j - 1, i)))
                for i in range(j, nb):
                    first = max(i, j + 1)
                    tasks.append((bottom - first, call(self.update, i, first, bottom - first)))
            for i in range(j + 1, bottom):
                tasks.append((0.2, call(self.split_column, j, i)))
            tasks += extra.get(j, [])
            w3 = right3(run(self.chain(j, w3), tasks))
        self.scale(w3, nb - 1, nb)


def scratch_for(nb, rhs):
    rows = nb * T + rhs
    return [
        pltpu.VMEM((rows, nb * T), F32),
        pltpu.VMEM((nb * T, 2 * WIDE), BF),
        pltpu.VMEM((nb * T, 2 * WIDE), BF),
        pltpu.VMEM((rows, 2 * T), BF),
        pltpu.VMEM((rows, 2 * T), BF),
    ]


def local(feat_ref, la_ref):
    a, lo = prep_local(feat_ref[...], feat_ref.shape[0])
    la_ref[0:WIDE, :] = a
    la_ref[WIDE:, :] = lo


def tile(fac, la_ref, t_ref, i):
    b = fac.b[blk(i), :]
    left = jnp.concatenate([b, b[:, :WIDE]], axis=1)
    right = jnp.concatenate([la_ref[0:WIDE, :], la_ref[...]], axis=0)
    hi, lo = split(jnp.exp((2.0 / fac.width) * mm(left, right)))
    t_ref[0, blk(i), :] = hi
    t_ref[1, blk(i), :] = lo


VM = pl.BlockSpec(memory_space=pltpu.VMEM)
SM = pl.BlockSpec(memory_space=pltpu.SMEM)


def onehot(ids_ref, me, per_dev, rows):
    row, lane = iota((per_dev, rows), 0), iota((per_dev, rows), 1)
    hot = jnp.zeros((per_dev, rows), F32)
    for i in range(per_dev):
        slot = ids_ref[0, me * per_dev + i] - me * rows
        hot = jnp.where((row == i) & (lane == slot), 1.0, hot)
    return hot


def own_kernel(per_dev, ids_ref, me_ref, feat_ref, targ_ref, out_ref):
    rows = feat_ref.shape[1]
    hot = onehot(ids_ref, me_ref[0], per_dev, rows)
    hot = jnp.concatenate([hot, jnp.zeros((128 - per_dev, rows), F32)], axis=0).astype(BF)
    both = jnp.concatenate(
        [feat_ref[...], targ_ref[...],
         jnp.zeros((LANES - feat_ref.shape[0] - targ_ref.shape[0], rows), F32)], axis=0)
    hi = both.astype(BF)
    rest = both - hi.astype(F32)
    mid = rest.astype(BF)
    low = (rest - mid.astype(F32)).astype(BF)
    picked = mm_nt(hi, hot) + mm_nt(mid, hot) + mm_nt(low, hot)
    out_ref[...] = picked.T[0:per_dev, :]


def own_rows(ids, me, feat_t, targ_t, per_dev):
    return pl.pallas_call(
        functools.partial(own_kernel, per_dev),
        out_shape=jax.ShapeDtypeStruct((per_dev, LANES), F32),
        in_specs=[SM, SM, VM, VM],
        out_specs=VM,
        name="own_rows",
    )(ids, me, feat_t, targ_t)


def step_kernel(per_dev, n_parts, ids_ref, me_ref, feat_ref, targ_ref, *refs):
    parts, refs = refs[:n_parts], refs[n_parts:]
    coef_ref, res_ref, t_ref, la_ref = refs[:4]
    refs = refs[4:]
    width, rows = feat_ref.shape
    classes = targ_ref.shape[0]
    nb = sum(p.shape[0] for p in parts) // T
    fac = Factor(width, nb, refs, parts)

    extra, at = {}, 0
    for j, count in enumerate((0, 0, 0, 0, 0, 2, 3, 3)):
        extra[j] = [(5.0, functools.partial(tile, fac, la_ref, t_ref, at + i)) for i in range(count)]
        at += count
    extra[4] = [(2.0, functools.partial(local, feat_ref, la_ref))]
    fac.go(extra)

    upd = jnp.zeros((RHS, rows), F32)
    s = fac.s
    low = fac.at(nb, 1)
    for k in range(nb - 1, -1, -1):
        x = s[low, blk(k)]
        x3 = left3(x)
        if k:
            s[low, blk(k - 1)] -= mm(x3, right3(s[blk(k), blk(k - 1)]))
        if k > 1:
            s[low, 0:(k - 1) * T] -= mm(x3, right3(s[blk(k), 0:(k - 1) * T]))
        t3 = jnp.concatenate([t_ref[0, blk(k), :], t_ref[0, blk(k), :], t_ref[1, blk(k), :]], axis=0)
        upd = upd + mm(x3, t3)

    first = width - (LANES - T) - RHS_AT
    hot = onehot(ids_ref, me_ref[0], per_dev, rows)
    hot = jnp.concatenate([hot, jnp.zeros((128 - per_dev, rows), F32)], axis=0)
    own = jnp.dot(x[:, 0:128], hot, precision=lax.Precision.HIGHEST, preferred_element_type=F32)
    own = own[first:first + classes]
    coef_ref[...] = own
    res_ref[...] = targ_ref[...] - upd[first:first + classes, :] - own


def solve_call(ids, me, feat_t, targ_t, parts, per_dev):
    nb = sum(p.shape[0] for p in parts) // T
    rows = feat_t.shape[1]
    args = [ids, me, feat_t, targ_t] + list(parts)
    return pl.pallas_call(
        functools.partial(step_kernel, per_dev, len(parts)),
        out_shape=[jax.ShapeDtypeStruct(targ_t.shape, F32)] * 2,
        in_specs=[SM, SM] + [VM] * (len(args) - 2),
        out_specs=[VM, VM],
        scratch_shapes=[pltpu.VMEM((2, nb * T, rows), BF), pltpu.VMEM((2 * WIDE, rows), BF)]
        + scratch_for(nb, RHS),
        compiler_params=pltpu.CompilerParams(vmem_limit_bytes=58 * 1024 * 1024),
        name="block_step",
    )(*args)


def place(x, y, z, core):
    return (((x % 2) * 4 + y) * 2 + core) * 16 + z * 2 + x // 2


def along(z_step=0, flip=0):
    return [
        (place(x, y, z, c), place(x, y, (z + z_step) % 8, c ^ flip))
        for x in range(4) for y in range(4) for z in range(8) for c in range(2)
    ]


def crossed(step, first):
    pairs = []
    for x in range(4):
        for y in range(4):
            for z in range(8):
                for c in range(2):
                    if (c == 0) == first:
                        to = place(x, (y + step) % 4, z, c)
                    else:
                        to = place((x + step) % 4, y, z, c)
                    pairs.append((place(x, y, z, c), to))
    return pairs


def send(a, pairs):
    return lax.ppermute(a, ("row", "col"), pairs)


def per_device(features, targets, block_ids):
    per_dev = block_ids.shape[1] // lax.axis_size(("row", "col"))
    me = jnp.reshape(lax.axis_index(("row", "col")), (1,))
    feat_t, targ_t = features.T, targets.T
    own = own_rows(block_ids, me, feat_t, targ_t, per_dev)
    near = jnp.concatenate([own, send(own, along(1)), send(own, along(7))], axis=0)
    line = jnp.concatenate([near, send(near, along(3)), send(near, along(5))[: 2 * per_dev]], axis=0)
    plane = jnp.concatenate([line] + [send(line, crossed(k, True)) for k in (1, 3, 2)], axis=0)
    twin = send(plane, along(0, 1))
    sides = [send(plane, crossed(k, False)) for k in (1, 3, 2)]
    twins = [send(side, along(0, 1)) for side in sides]
    parts = [plane, twin] + sides[:2] + twins[:2] + sides[2:] + twins[2:]
    coef_t, res_t = solve_call(block_ids, me, feat_t, targ_t, parts, per_dev)
    return coef_t.T, res_t.T


def solution(mesh):
    spec = P(("row", "col"), None)
    return jax.shard_map(
        per_device, mesh=mesh, in_specs=(spec, spec, P()), out_specs=(spec, spec), check_vma=False
    )
```

```python
import functools

import jax
import jax.numpy as jnp
from jax import lax
from jax.experimental import pallas as pl
from jax.experimental.pallas import tpu as pltpu
from jax.sharding import PartitionSpec as P

BF, F32 = jnp.bfloat16, jnp.float32
T = 256
WIDE = 512
LANES = 640
LATE = 2
RHS_AT, RHS = 48, 160


def split(x):
    hi = x.astype(BF)
    return hi, (x - hi.astype(F32)).astype(BF)


def left3(x):
    hi, lo = split(x)
    return jnp.concatenate([hi, lo, hi], axis=1)


def right3(x):
    hi, lo = split(x)
    return jnp.concatenate([hi, hi, lo], axis=0)


def mm(a, b):
    return jnp.dot(a, b, preferred_element_type=F32)


def mm_nt(a, b, precision=None):
    return lax.dot_general(a, b, (((1,), (1,)), ((), ())), precision=precision, preferred_element_type=F32)


def iota(shape, dim):
    return lax.broadcasted_iota(jnp.int32, shape, dim)


def eye_mask():
    return iota((T, T), 0) == iota((T, T), 1)


def inverse(block):
    eye = jnp.where(eye_mask(), 1.0, 0.0).astype(F32)
    low, high = 1.0, 1.0 + T
    delta = (high - low) / (high + low)
    c0 = 2.0 / (high + low)
    r = eye - c0 * block
    x = None
    for step in range(6):
        c = 2.0 / (2.0 - delta * delta)
        if step == 4:
            rb = r.astype(BF)
            sq, more = mm(rb, rb), mm(x.astype(BF), rb)
            yield
            x = c * (x + more)
            r = (1.0 - c) * eye + c * sq
        elif step < 5:
            rr = right3(r)
            sq = mm(left3(r), rr)
            more = None if x is None else mm(left3(x), rr)
            yield
            x = (c * c0) * (eye + r) if x is None else c * (x + more)
            r = (1.0 - c) * eye + c * sq
        else:
            more = mm(x.astype(BF), r.astype(BF))
            yield
            x = c * (x + more)
        delta = delta * delta / (2.0 - delta * delta)
    prod = mm(left3(block), right3(x))
    yield
    fix = eye - prod
    more = mm(x.astype(BF), fix.astype(BF))
    yield
    return x + more


SLOTS = 10


def run(chain, tasks):
    total = sum(cost for cost, _ in tasks)
    tasks = list(tasks)
    done, at = 0.0, 0
    while True:
        try:
            next(chain)
        except StopIteration as stop:
            for _, task in tasks:
                task()
            return stop.value
        at += 1
        while tasks and done < total * at / SLOTS:
            cost, task = tasks.pop(0)
            task()
            done += cost


def spare(half, one):
    s1 = half.astype(BF).astype(F32)
    s2 = (half - s1).astype(BF).astype(F32)
    s3 = (half - s1 - s2).astype(BF).astype(F32)
    return [(s1, one), (s2, one), (s3, one), (one, s1), (one, s2), (one, s3)]


def prep_rows(f, width):
    base = width // 128 * 128
    main, tail = f[:, :base], f[:, base:]
    lane = iota(tail.shape, 1) + base
    tail = jnp.where(lane < width, tail, 0.0)
    half = -0.5 * (jnp.sum(main * main, axis=1, keepdims=True) + jnp.sum(tail * tail, axis=1, keepdims=True))
    hi, lo = split(main)
    tail_hi, tail_lo = split(tail)
    a = b = tail_hi.astype(F32)
    for n, (va, vb) in enumerate(spare(half, jnp.ones_like(half))):
        a = jnp.where(lane == width + n, va, a)
        b = jnp.where(lane == width + n, vb, b)
    join = lambda p, q: jnp.concatenate([p, q], axis=1)
    return join(hi, a.astype(BF)), join(hi, b.astype(BF)), join(lo, tail_lo)


def prep_local(ft, width):
    f = jnp.concatenate([ft, jnp.zeros((WIDE - width, ft.shape[1]), F32)], axis=0)
    row = iota(f.shape, 0)
    half = -0.5 * jnp.sum(f * f, axis=0, keepdims=True)
    hi, lo = split(f)
    a = hi.astype(F32)
    for n, (va, _) in enumerate(spare(half, jnp.ones_like(half))):
        a = jnp.where(row == width + n, va, a)
    return a.astype(BF), lo


def blk(i, count=1):
    return slice(i * T, (i + count) * T)


class Factor:
    def __init__(self, width, nb, refs, parts):
        self.width, self.nb, self.parts = width, nb, parts
        self.s, self.a, self.b, self.q, self.g = refs

    def at(self, first, count):
        stop = (first + count) * T
        return slice(first * T, self.nb * T + RHS if stop > self.nb * T else stop)

    def rows_of(self, i):
        for part in self.parts:
            count = part.shape[0] // T
            if i < count:
                return part, blk(i)
            i -= count
        raise IndexError(i)

    def prep(self, i):
        if i in self.late:
            self.late[i].wait()
        part, at = self.rows_of(i)
        a, b, lo = prep_rows(part[at, 0:WIDE], self.width)
        for ref, hi in ((self.a, a), (self.b, b)):
            ref[blk(i), 0:WIDE] = hi
            ref[blk(i), WIDE:] = lo
        self.s[self.nb * T:, blk(i)] = part[at, LANES - T:].T[RHS_AT:RHS_AT + RHS]

    def gram(self, i, first, count):
        left = self.a[blk(first, count), :]
        left = jnp.concatenate([left, left[:, :WIDE]], axis=1)
        b = self.b[blk(i), :]
        right = jnp.concatenate([b[:, :WIDE], b], axis=1)
        g = jnp.exp((2.0 / self.width) * mm_nt(left, right))
        if first == i:
            self.s[blk(i), blk(i)] = jnp.where(eye_mask(), 2.0, g[:T])
            first, count, g = first + 1, count - 1, g[T:]
        if count:
            self.s[blk(first, count), blk(i)] = g

    def split_column(self, j, i):
        hi, lo = split(self.s[self.at(i, 1), blk(j)])
        self.q[self.at(i, 1), 0:T] = hi
        self.q[self.at(i, 1), T:] = lo

    def q3(self, first, count):
        q = self.q[self.at(first, count), :]
        return jnp.concatenate([q, q[:, :T]], axis=1)

    def scale(self, w3, j, i):
        g = mm(self.q3(i, 1), w3)
        hi, lo = split(g)
        self.g[self.at(i, 1), 0:T] = hi
        self.g[self.at(i, 1), T:] = lo
        self.s[self.at(i, 1), blk(j)] = g

    def update(self, i, first, count):
        g = self.g[blk(i), :]
        right = jnp.concatenate([g[:, :T], g], axis=1)
        self.s[self.at(first, count), blk(i)] -= mm_nt(self.q3(first, count), right)

    def chain(self, j, w3):
        if j:
            self.scale(w3, j - 1, j)
            yield
            self.update(j, j, 1)
            yield
        else:
            self.prep(0)
            yield
            self.gram(0, 0, 1)
            yield
        block = self.s[blk(j), blk(j)]
        w = yield from inverse(block)
        return w

    def go(self, extra):
        nb, bottom = self.nb, self.nb + 1
        call = functools.partial
        w3 = None
        for j in range(nb):
            tasks = []
            if j == 0:
                for i in range(1, nb):
                    tasks.append((0.6, call(self.prep, i)))
                tasks.append((2.0 * (nb - 1), call(self.gram, 0, 1, nb - 1)))
                for i in range(1, nb):
                    tasks.append((2.0 * (nb - i), call(self.gram, i, i, nb - i)))
            else:
                for i in range(j + 1, bottom):
                    tasks.append((1.2, call(self.scale, w3, j - 1, i)))
                for i in range(j, nb):
                    first = max(i, j + 1)
                    tasks.append((bottom - first, call(self.update, i, first, bottom - first)))
            for i in range(j + 1, bottom):
                tasks.append((0.2, call(self.split_column, j, i)))
            tasks += extra.get(j, [])
            w3 = right3(run(self.chain(j, w3), tasks))
        self.scale(w3, nb - 1, nb)


def scratch_for(nb, rhs):
    rows = nb * T + rhs
    return [
        pltpu.VMEM((rows, nb * T), F32),
        pltpu.VMEM((nb * T, 2 * WIDE), BF),
        pltpu.VMEM((nb * T, 2 * WIDE), BF),
        pltpu.VMEM((rows, 2 * T), BF),
        pltpu.VMEM((rows, 2 * T), BF),
    ]


def local(feat_ref, la_ref):
    a, lo = prep_local(feat_ref[...], feat_ref.shape[0])
    la_ref[0:WIDE, :] = a
    la_ref[WIDE:, :] = lo


def tile(fac, la_ref, t_ref, i):
    b = fac.b[blk(i), :]
    left = jnp.concatenate([b, b[:, :WIDE]], axis=1)
    right = jnp.concatenate([la_ref[0:WIDE, :], la_ref[...]], axis=0)
    hi, lo = split(jnp.exp((2.0 / fac.width) * mm(left, right)))
    t_ref[0, blk(i), :] = hi
    t_ref[1, blk(i), :] = lo


VM = pl.BlockSpec(memory_space=pltpu.VMEM)
SM = pl.BlockSpec(memory_space=pltpu.SMEM)


def onehot(ids_ref, me, per_dev, rows):
    row, lane = iota((per_dev, rows), 0), iota((per_dev, rows), 1)
    hot = jnp.zeros((per_dev, rows), F32)
    for i in range(per_dev):
        slot = ids_ref[0, me * per_dev + i] - me * rows
        hot = jnp.where((row == i) & (lane == slot), 1.0, hot)
    return hot


def own_kernel(per_dev, ids_ref, me_ref, feat_ref, targ_ref, out_ref):
    rows = feat_ref.shape[1]
    hot = onehot(ids_ref, me_ref[0], per_dev, rows)
    hot = jnp.concatenate([hot, jnp.zeros((128 - per_dev, rows), F32)], axis=0).astype(BF)
    both = jnp.concatenate(
        [feat_ref[...], targ_ref[...],
         jnp.zeros((LANES - feat_ref.shape[0] - targ_ref.shape[0], rows), F32)], axis=0)
    hi = both.astype(BF)
    rest = both - hi.astype(F32)
    mid = rest.astype(BF)
    low = (rest - mid.astype(F32)).astype(BF)
    picked = mm_nt(hi, hot) + mm_nt(mid, hot) + mm_nt(low, hot)
    out_ref[...] = picked.T[0:per_dev, :]


def own_rows(ids, me, feat_t, targ_t, per_dev):
    return pl.pallas_call(
        functools.partial(own_kernel, per_dev),
        out_shape=jax.ShapeDtypeStruct((per_dev, LANES), F32),
        in_specs=[SM, SM, VM, VM],
        out_specs=VM,
        name="own_rows",
    )(ids, me, feat_t, targ_t)


def step_kernel(per_dev, n_parts, ids_ref, me_ref, feat_ref, targ_ref, *refs):
    parts, late, refs = refs[:n_parts - LATE], refs[n_parts - LATE:n_parts], refs[n_parts:]
    coef_ref, res_ref, t_ref, la_ref, held, sems = refs[:6]
    refs = refs[6:]
    copies = [pltpu.make_async_copy(src, held.at[i], sems.at[i]) for i, src in enumerate(late)]
    for copy in copies:
        copy.start()
    parts = list(parts) + [held.at[i] for i in range(LATE)]
    width, rows = feat_ref.shape
    classes = targ_ref.shape[0]
    nb = sum(p.shape[0] for p in parts) // T
    fac = Factor(width, nb, refs, parts)
    fac.late = {nb - LATE + i: copy for i, copy in enumerate(copies)}

    extra, at = {}, 0
    for j, count in enumerate((0, 0, 0, 0, 0, 2, 3, 3)):
        extra[j] = [(5.0, functools.partial(tile, fac, la_ref, t_ref, at + i)) for i in range(count)]
        at += count
    extra[4] = [(2.0, functools.partial(local, feat_ref, la_ref))]
    fac.go(extra)

    upd = jnp.zeros((RHS, rows), F32)
    s = fac.s
    low = fac.at(nb, 1)
    for k in range(nb - 1, -1, -1):
        x = s[low, blk(k)]
        x3 = left3(x)
        if k:
            s[low, blk(k - 1)] -= mm(x3, right3(s[blk(k), blk(k - 1)]))
        if k > 1:
            s[low, 0:(k - 1) * T] -= mm(x3, right3(s[blk(k), 0:(k - 1) * T]))
        t3 = jnp.concatenate([t_ref[0, blk(k), :], t_ref[0, blk(k), :], t_ref[1, blk(k), :]], axis=0)
        upd = upd + mm(x3, t3)

    first = width - (LANES - T) - RHS_AT
    hot = onehot(ids_ref, me_ref[0], per_dev, rows)
    hot = jnp.concatenate([hot, jnp.zeros((128 - per_dev, rows), F32)], axis=0)
    own = jnp.dot(x[:, 0:128], hot, precision=lax.Precision.HIGHEST, preferred_element_type=F32)
    own = own[first:first + classes]
    coef_ref[...] = own
    res_ref[...] = targ_ref[...] - upd[first:first + classes, :] - own


def solve_call(ids, me, feat_t, targ_t, parts, per_dev):
    nb = sum(p.shape[0] for p in parts) // T
    rows = feat_t.shape[1]
    args = [ids, me, feat_t, targ_t] + list(parts)
    return pl.pallas_call(
        functools.partial(step_kernel, per_dev, len(parts)),
        out_shape=[jax.ShapeDtypeStruct(targ_t.shape, F32)] * 2,
        in_specs=[SM, SM] + [VM] * (len(args) - 2 - LATE) + [pl.BlockSpec(memory_space=pltpu.HBM)] * LATE,
        out_specs=[VM, VM],
        scratch_shapes=[pltpu.VMEM((2, nb * T, rows), BF), pltpu.VMEM((2 * WIDE, rows), BF),
                        pltpu.VMEM((LATE, T, LANES), F32), pltpu.SemaphoreType.DMA((LATE,))]
        + scratch_for(nb, RHS),
        compiler_params=pltpu.CompilerParams(vmem_limit_bytes=58 * 1024 * 1024),
        name="block_step",
    )(*args)


def place(x, y, z, core):
    return (((x % 2) * 4 + y) * 2 + core) * 16 + z * 2 + x // 2


def along(z_step=0, flip=0):
    return [
        (place(x, y, z, c), place(x, y, (z + z_step) % 8, c ^ flip))
        for x in range(4) for y in range(4) for z in range(8) for c in range(2)
    ]


def crossed(step, first):
    pairs = []
    for x in range(4):
        for y in range(4):
            for z in range(8):
                for c in range(2):
                    if (c == 0) == first:
                        to = place(x, (y + step) % 4, z, c)
                    else:
                        to = place((x + step) % 4, y, z, c)
                    pairs.append((place(x, y, z, c), to))
    return pairs


def send(a, pairs):
    return lax.ppermute(a, ("row", "col"), pairs)


def per_device(features, targets, block_ids):
    per_dev = block_ids.shape[1] // lax.axis_size(("row", "col"))
    me = jnp.reshape(lax.axis_index(("row", "col")), (1,))
    feat_t, targ_t = features.T, targets.T
    own = own_rows(block_ids, me, feat_t, targ_t, per_dev)
    near = jnp.concatenate([own, send(own, along(1)), send(own, along(7))], axis=0)
    line = jnp.concatenate([near, send(near, along(3)), send(near, along(5))[: 2 * per_dev]], axis=0)
    plane = jnp.concatenate([line] + [send(line, crossed(k, True)) for k in (1, 3, 2)], axis=0)
    twin = send(plane, along(0, 1))
    sides = [send(plane, crossed(k, False)) for k in (1, 3, 2)]
    twins = [send(side, along(0, 1)) for side in sides]
    parts = [plane, twin] + sides[2:] + twins[2:] + sides[:2] + twins[:2]
    coef_t, res_t = solve_call(block_ids, me, feat_t, targ_t, parts, per_dev)
    return coef_t.T, res_t.T


def solution(mesh):
    spec = P(("row", "col"), None)
    return jax.shard_map(
        per_device, mesh=mesh, in_specs=(spec, spec, P()), out_specs=(spec, spec), check_vma=False
    )
```
